32 devices in a mesh: sub: 8 (over z, y), grp: 4 (over x, core).
Axes of the slice: x: 2, y: 2, z: 4, core: 2. Of those that a mesh axis runs over, the one named last changes fastest.
Arguments:
- right_side: float32 [512, 8192], P('grp', 'sub'), may hold values from -6 to 6
- operator_block: bfloat16 [8192, 1024], P('sub'), may hold values from -0.1875 to 0.1875
- operator_diag: float32 [8192], P('sub'), may hold values from 2 to 4
- solve_block: bfloat16 [8192, 1024], P('sub'), may hold values from -0.1875 to 0.1875
- solve_diag: float32 [8192], P('sub'), may hold values from 0.5 to 1.5
- upper_rows: int32 [8, 128], P('sub'), may hold values from 0 to 1023, as said below
- lower_rows: int32 [8, 128], P('sub'), may hold values from 0 to 1023, as said below
- couple_up: bfloat16 [1024, 128], P('sub'), may hold values from -0.5 to 0.5
- couple_down: bfloat16 [1024, 128], P('sub'), may hold values from -0.5 to 0.5
- coarse_basis: bfloat16 [64, 8192], P(None, 'sub'), may hold values from -0.75 to 0.75
- coarse_inverse: bfloat16 [512, 512], P(('sub', 'grp')), may hold values from -0.046875 to 0.046875
Outputs:
- solution: float32 [512, 8192], P('grp', 'sub')
The draws below stay inside these ranges and needn't reach their ends.
Inputs may be any that keep to these rules, and one draw needn't show every extreme that they name: `upper_rows`: local row numbers within a subdomain of 1024 unknowns; the 128 entries of one subdomain are distinct, and none of them appears in lower_rows of the same subdomain. `lower_rows`: local row numbers within a subdomain of 1024 unknowns; the 128 entries of one subdomain are distinct, and none of them appears in upper_rows of the same subdomain.
All inputs are finite; a program needn't handle non-finite values.
Results may differ from the reference program's by a relative error of at most 0.0042.
Values may be sent and summed in bfloat16 or wider, within the bound.
A program may use at most 64 MiB of HBM per device.

```python
import jax
import jax.numpy as jnp
from jax import lax

SUBS = 8
NLOC = 1024
NRHS = 512
KC = 64
ITERS = 3
FACE = 128
NTOT = 8192
NCOARSE = 512
N_SUB = 8


def face_orders(key):
    keys = jax.random.split(jax.random.fold_in(key, 11), SUBS)
    return jax.vmap(lambda single: jax.random.permutation(single, NLOC))(keys).astype(jnp.int32)


def draw_upper_rows(key, part):
    return face_orders(key)[:, :FACE]


def draw_lower_rows(key, part):
    return face_orders(key)[:, FACE:2 * FACE]


def block_scale(key, shape, cuts, least, high):
    factor_of, own = 1.0, jax.random.fold_in(key, 6)
    for axis_at, parts in cuts:
        draws = jnp.exp(jax.random.uniform(jax.random.fold_in(own, axis_at), (parts,), jnp.float32, least / len(cuts), high / len(cuts)))
        factor_of = factor_of * jnp.repeat(draws, shape[axis_at] // parts).reshape([-1 if axis == axis_at else 1 for axis in range(len(shape))])
    return factor_of


def centred(key, shape, deviation, most, pieces=(), kind=jnp.bfloat16):
    values = deviation * jax.random.normal(key, shape, jnp.float32)
    if pieces:
        values = values * block_scale(key, shape, pieces, -0.22, 0.18)
    return jnp.clip(values, -most, most).astype(kind)


def setup_inputs(seed: int = 0) -> dict:
    splits = jax.random.split(jax.random.key(seed), 12)
    return {
        "right_side": centred(splits[0], (NRHS, NTOT), 1.0, 6.0, ((0, 4), (1, 8)), jnp.float32),
        "operator_block": centred(splits[1], (NTOT, NLOC), NLOC ** -0.5, 0.1875, ((0, 8),)),
        "operator_diag": jnp.clip(2.0 + 2.0 * jax.random.uniform(splits[2], (NTOT,), jnp.float32) ** block_scale(splits[2], (NTOT,), ((0, 8),), -0.2, 0.2), 2.0, 4.0),
        "solve_block": centred(splits[3], (NTOT, NLOC), NLOC ** -0.5, 0.1875, ((0, 8),)),
        "solve_diag": jnp.clip(0.5 + 1.0 * jax.random.uniform(splits[4], (NTOT,), jnp.float32) ** block_scale(splits[4], (NTOT,), ((0, 8),), -0.2, 0.2), 0.5, 1.5),
        "upper_rows": draw_upper_rows(jax.random.fold_in(splits[11], 71), 0),
        "lower_rows": draw_lower_rows(jax.random.fold_in(splits[11], 71), 0),
        "couple_up": centred(splits[7], (SUBS * FACE, FACE), FACE ** -0.5, 0.5, ((0, 8),)),
        "couple_down": centred(splits[8], (SUBS * FACE, FACE), FACE ** -0.5, 0.5, ((0, 8),)),
        "coarse_basis": centred(splits[9], (KC, NTOT), KC ** -0.5, 0.75, ((1, 8),)),
        "coarse_inverse": centred(splits[10], (NCOARSE, NCOARSE), (32 * NCOARSE) ** -0.5, 0.046875, ((0, 32),)),
    }


EPS = 1e-06

def contract_last(left, right):
    return lax.dot_general(left, right, (((1,), (1,)), ((), ())), preferred_element_type=jnp.float32)

def block_products(vector_b, stacked):
    per_sub = vector_b.reshape(NRHS, N_SUB, NLOC).transpose(1, 0, 2)
    matrices = stacked.reshape(N_SUB, NLOC, NLOC)
    product = lax.map(lambda couple_pair: contract_last(couple_pair[0], couple_pair[1]), (per_sub, matrices))
    return product.transpose(1, 0, 2).reshape(NRHS, N_SUB * NLOC)

def apply_operator(vector, operator_block, operator_diag, upper_rows, lower_rows, couple_up, couple_down):
    face_count = NLOC // 8
    vector_b = vector.astype(jnp.bfloat16)
    product = block_products(vector_b, operator_block)
    by_sub = vector_b.reshape(NRHS, N_SUB, NLOC)
    upper_idx = upper_rows.reshape(N_SUB, face_count).astype(jnp.int32)
    lower_idx = lower_rows.reshape(N_SUB, face_count).astype(jnp.int32)
    shape_full = (NRHS, N_SUB, face_count)
    up_face = jnp.take_along_axis(by_sub, jnp.broadcast_to(upper_idx[None], shape_full), axis=2)
    low_face = jnp.take_along_axis(by_sub, jnp.broadcast_to(lower_idx[None], shape_full), axis=2)
    from_below = jnp.roll(up_face, 1, axis=1).astype(jnp.float32)
    from_above = jnp.roll(low_face, -1, axis=1).astype(jnp.float32)
    coupling_up = couple_up.reshape(N_SUB, face_count, face_count).astype(jnp.float32)
    coupling_down = couple_down.reshape(N_SUB, face_count, face_count).astype(jnp.float32)
    into_upper = jnp.einsum('rse,sef->rsf', from_above, coupling_up)
    into_lower = jnp.einsum('rse,sef->rsf', from_below, coupling_down)
    positions = jnp.arange(NLOC, dtype=jnp.int32)
    onehot_up = (upper_idx[..., None] == positions).astype(jnp.float32)
    onehot_low = (lower_idx[..., None] == positions).astype(jnp.float32)
    face_terms = jnp.einsum('rsf,sfm->rsm', into_upper, onehot_up) + jnp.einsum('rsf,sfm->rsm', into_lower, onehot_low)
    return operator_diag[None, :] * vector + product + face_terms.reshape(NRHS, N_SUB * NLOC)

def apply_solve(vector, solve_block, solve_diag, coarse_basis, coarse_inverse):
    vector_b = vector.astype(jnp.bfloat16)
    local_term = block_products(vector_b, solve_block)
    basis_f = coarse_basis.reshape(KC, N_SUB, NLOC).astype(jnp.float32)
    vector_f = vector_b.reshape(NRHS, N_SUB, NLOC).astype(jnp.float32)
    coarse_res = jnp.einsum('ksn,rsn->skr', basis_f, vector_f).reshape(N_SUB * KC, NRHS).astype(jnp.bfloat16)
    solved = jnp.dot(coarse_inverse, coarse_res, preferred_element_type=jnp.float32).astype(jnp.bfloat16)
    solved_f = solved.reshape(N_SUB, KC, NRHS).astype(jnp.float32)
    coarse_term = jnp.einsum('skr,ksn->rsn', solved_f, basis_f).reshape(NRHS, N_SUB * NLOC)
    return solve_diag[None, :] * vector + local_term + coarse_term

def least_squares(initial_norm, columns):
    extent = len(columns)
    rotations = []
    target = [initial_norm] + [jnp.zeros_like(initial_norm) for _ in range(extent)]
    triangle = []
    for j in range(extent):
        column = list(columns[j])
        for i in range(j):
            cosine, sine_value = rotations[i]
            leading = cosine * column[i] + sine_value * column[i + 1]
            column[i + 1] = -sine_value * column[i] + cosine * column[i + 1]
            column[i] = leading
        radius = jnp.sqrt(column[j] * column[j] + column[j + 1] * column[j + 1])
        cosine = column[j] / radius
        sine_value = column[j + 1] / radius
        column[j] = radius
        rotations.append((cosine, sine_value))
        target[j + 1] = -sine_value * target[j]
        target[j] = cosine * target[j]
        triangle.append(column[:j + 1])
    coeffs = [None] * extent
    for j in reversed(range(extent)):
        partial_sum = target[j]
        for k in range(j + 1, extent):
            partial_sum = partial_sum - triangle[k][j] * coeffs[k]
        coeffs[j] = partial_sum / triangle[j][j]
    return coeffs

def reference(right_side, operator_block, operator_diag, solve_block, solve_diag, upper_rows, lower_rows, couple_up, couple_down, coarse_basis, coarse_inverse):

    def operator(vector):
        return apply_operator(vector, operator_block, operator_diag, upper_rows, lower_rows, couple_up, couple_down)

    def precond(vector):
        return apply_solve(vector, solve_block, solve_diag, coarse_basis, coarse_inverse)

    def norm_of(vector):
        return jnp.sqrt(lax.optimization_barrier(jnp.sum(vector * vector, axis=1)) + EPS)
    residual = precond(right_side)
    initial_norm = norm_of(residual)
    krylov = [residual / initial_norm[:, None]]
    columns = []
    for iteration in range(ITERS):
        candidate = precond(operator(krylov[iteration]))
        heights = [lax.optimization_barrier(jnp.sum(candidate * krylov[i], axis=1)) for i in range(iteration + 1)]
        for i in range(iteration + 1):
            candidate = candidate - heights[i][:, None] * krylov[i]
        height = norm_of(candidate)
        heights.append(height)
        krylov.append(candidate / height[:, None])
        columns.append(heights)
    coeffs = least_squares(initial_norm, columns)
    solution = coeffs[0][:, None] * krylov[0]
    for j in range(1, ITERS):
        solution = solution + coeffs[j][:, None] * krylov[j]
    return solution
```

```python
import functools

import jax
import jax.numpy as jnp
from jax import lax
from jax.experimental import pallas as pl
from jax.experimental.pallas import tpu as pltpu
from jax.sharding import PartitionSpec as P

ITERS = 3
EPS = 1e-06
TILE = 256
MESH = pl.DeviceIdType.MESH
BF = jnp.bfloat16
F32 = jnp.float32


def dot(a, b):
    return jnp.dot(a, b, preferred_element_type=F32)


def least_squares(initial_norm, columns):
    extent = len(columns)
    rotations = []
    target = [initial_norm] + [jnp.zeros_like(initial_norm) for _ in range(extent)]
    triangle = []
    for j in range(extent):
        column = list(columns[j])
        for i in range(j):
            cosine, sine_value = rotations[i]
            leading = cosine * column[i] + sine_value * column[i + 1]
            column[i + 1] = -sine_value * column[i] + cosine * column[i + 1]
            column[i] = leading
        radius = jnp.sqrt(column[j] * column[j] + column[j + 1] * column[j + 1])
        cosine = column[j] / radius
        sine_value = column[j + 1] / radius
        column[j] = radius
        rotations.append((cosine, sine_value))
        target[j + 1] = -sine_value * target[j]
        target[j] = cosine * target[j]
        triangle.append(column[: j + 1])
    coeffs = [None] * extent
    for j in reversed(range(extent)):
        partial_sum = target[j]
        for k in range(j + 1, extent):
            partial_sum = partial_sum - triangle[k][j] * coeffs[k]
        coeffs[j] = partial_sum / triangle[j][j]
    return coeffs


def each_peer(count, body):
    if count <= 8:
        for k in range(1, count):
            body(k)
    else:
        def step(k, carry):
            body(k)
            return carry
        lax.fori_loop(1, count, step, 0)


def kernel(
    n, g, rhs_h, op_h, od_h, sv_h, sd_h, up_h, lo_h, cu_h, cd_h, cb_h, ci_h, out_h,
    rhs_v, op_v, od_v, sv_v, sd_v, up_v, lo_v, cu_v, cd_v, cb_v, ci_v,
    odt, sdt, pg, ct, cbt, w, wb, vs, al, u, ub, loc, out_v,
    yall, fout, fin, vf, dall,
    in_sem, out_sem, ci_sem, ysem, fsem, dsem,
):
    me = lax.axis_index("sub")
    mg = lax.axis_index("grp")
    nloc = op_v.shape[0]
    kc = cb_v.shape[0]
    face = up_v.shape[1]
    part = ci_h.shape[0]
    tiles = nloc // TILE

    def rows(t):
        return pl.ds(t * TILE, TILE)

    loads = [
        pltpu.make_async_copy(src, dst, in_sem.at[i])
        for i, (src, dst) in enumerate([
            (rhs_h, rhs_v), (cb_h, cb_v), (sv_h, sv_v), (op_h, op_v), (od_h, od_v), (sd_h, sd_v),
            (up_h, up_v), (lo_h, lo_v), (cu_h, cu_v), (cd_h, cd_v),
            (ci_h, ci_v.at[pl.ds(pl.multiple_of(mg * part, part), part)]),
        ])
    ]
    for load in loads:
        load.start()

    barrier = pltpu.get_barrier_semaphore()
    each_peer(n, lambda k: pl.semaphore_signal(
        barrier, inc=1, device_id={"sub": lax.rem(me + k, n)}, device_id_type=MESH))
    each_peer(g, lambda k: pl.semaphore_signal(
        barrier, inc=1, device_id={"grp": lax.rem(mg + k, g)}, device_id_type=MESH))

    loads[0].wait()
    for t in range(tiles):
        tile = rhs_v[:, rows(t)].T
        u[rows(t), :] = tile
        ub[rows(t), :] = tile.astype(BF)
    loads[1].wait()
    loads[10].wait()

    pl.semaphore_wait(barrier, n - 1 + g - 1)

    my_part = pl.ds(pl.multiple_of(mg * part, part), part)

    def send_part(k):
        pltpu.make_async_remote_copy(
            ci_v.at[my_part], ci_v.at[my_part], ci_sem.at[0], ci_sem.at[1],
            device_id={"grp": lax.rem(mg + k, g)}, device_id_type=MESH).start()

    def y_start(p):
        slot = pl.ds(pl.multiple_of(me * kc, kc), kc)
        yall[p, slot, :] = dot(cb_v[...], ub[...]).astype(BF)

        def send(k):
            pltpu.make_async_remote_copy(
                yall.at[p, slot], yall.at[p, slot], ysem.at[p, 0], ysem.at[p, 1],
                device_id={"sub": lax.rem(me + k, n)}, device_id_type=MESH).start()
        each_peer(n, send)

    def y_wait(p, which):
        span = yall.at[p, pl.ds(0, (n - 1) * kc)]
        pltpu.make_async_copy(span, span, ysem.at[p, which]).wait()

    def d_wait(p, which):
        span = dall.at[p, pl.ds(0, (n - 1) * 8)]
        pltpu.make_async_copy(span, span, dsem.at[p, which]).wait()

    def ci_wait(which):
        span = ci_v.at[pl.ds(0, (g - 1) * part)]
        pltpu.make_async_copy(span, span, ci_sem.at[which]).wait()

    def face_copies(p):
        down = {"sub": lax.rem(me + n - 1, n)}
        up = {"sub": lax.rem(me + 1, n)}
        lower = pltpu.make_async_remote_copy(
            fout.at[p, pl.ds(face, face)], fin.at[p, pl.ds(0, face)],
            fsem.at[p, 0], fsem.at[p, 1], device_id=down, device_id_type=MESH)
        upper = pltpu.make_async_remote_copy(
            fout.at[p, pl.ds(0, face)], fin.at[p, pl.ds(face, face)],
            fsem.at[p, 2], fsem.at[p, 3], device_id=up, device_id_type=MESH)
        return lower, upper

    y_start(0)
    each_peer(g, send_part)

    for load in loads[4:10]:
        load.wait()
    for t in range(tiles):
        cols = rows(t)
        sdt[cols, :] = jnp.broadcast_to(sd_v[:, cols], (128, TILE)).T
        odt[cols, :] = jnp.broadcast_to(od_v[:, cols], (128, TILE)).T
        cbt[cols, :] = cb_v[:, cols].astype(F32).T.astype(BF)
        position = lax.broadcasted_iota(jnp.int32, (TILE, face), 0) + t * TILE
        for f, (list_v, couple_v) in enumerate(((up_v, cu_v), (lo_v, cd_v))):
            hot = (position == jnp.broadcast_to(list_v[...], (TILE, face))).astype(F32)
            pg[pl.ds(f * face, face), cols] = hot.T.astype(BF)
            ct[cols, pl.ds(f * face, face)] = lax.dot_general(
                hot.astype(BF), couple_v[...], (((1,), (1,)), ((), ())),
                preferred_element_type=F32).astype(BF)
    loads[2].wait()

    heights = []
    gram = {}
    initial_norm = None
    for j in range(-1, ITERS):
        p = j + 1
        for t in range(tiles):
            loc[rows(t), :] = sdt[rows(t), :] * u[rows(t), :] + dot(sv_v[rows(t), :], ub[...])
        if p == 0 and g > 1:
            ci_wait(1)
        y_wait(p, 1)
        c = dot(ci_v[...], yall[p]).astype(BF)
        sums = [None] * (2 * p + 1)
        for t in range(tiles):
            tile = loc[rows(t), :] + dot(cbt[rows(t), :], c)
            w[rows(t), :] = tile
            if j < ITERS - 1:
                high = tile.astype(BF)
                wb[rows(t), 0:128] = high
                wb[rows(t), 128:256] = (tile - high.astype(F32)).astype(BF)
            pairs = [(tile, tile)]
            basis = [vs[i, rows(t), :] for i in range(p)]
            pairs += [(tile, b) for b in basis]
            pairs += [(basis[p - 1], b) for b in basis]
            for i, (a, b) in enumerate(pairs):
                one = jnp.sum((a * b).reshape(TILE // 8, 8, 128), axis=0)
                sums[i] = one if sums[i] is None else sums[i] + one
        packed = [jnp.sum(s, axis=0, keepdims=True) for s in sums]
        packed += [jnp.zeros((8 - len(packed), 128), F32)]
        slot = pl.ds(pl.multiple_of(me * 8, 8), 8)
        dall[p, slot, :] = jnp.concatenate(packed, axis=0)

        def send_dots(k):
            pltpu.make_async_remote_copy(
                dall.at[p, slot], dall.at[p, slot], dsem.at[p, 0], dsem.at[p, 1],
                device_id={"sub": lax.rem(me + k, n)}, device_id_type=MESH).start()
        each_peer(n, send_dots)

        if j < ITERS - 1:
            fout[p] = dot(pg[...], wb[:, 0:128]).astype(BF)
            for copy in face_copies(p):
                copy.start()
            if p == 0:
                loads[3].wait()
            for t in range(tiles):
                both = dot(op_v[rows(t), :], wb[...])
                al[p, rows(t), :] = odt[rows(t), :] * w[rows(t), :] + (both[:, :128] + both[:, 128:])

        d_wait(p, 1)
        total = jnp.sum(dall[p].reshape(n, 8, 128), axis=0)
        square = total[0:1, :]
        h = [total[1 + i:2 + i, :] for i in range(p)]
        for i in range(p):
            gram[i, p - 1] = gram[p - 1, i] = total[1 + p + i:2 + p + i, :]
        for i in range(p):
            square = square - 2.0 * h[i] * h[i]
            for k in range(p):
                square = square + h[i] * h[k] * gram[i, k]
        norm = jnp.sqrt(jnp.maximum(square, 0.0) + EPS)
        if p == 0:
            initial_norm = norm
        else:
            heights.append(h + [norm])
        if j == ITERS - 1:
            break
        scale = 1.0 / norm

        def orthogonal(value, earlier):
            for i in range(p):
                value = value - h[i] * earlier(i)
            return value * scale

        for t in range(tiles):
            vs[p, rows(t), :] = orthogonal(w[rows(t), :], lambda i: vs[i, rows(t), :])
            al[p, rows(t), :] = orthogonal(al[p, rows(t), :], lambda i: al[i, rows(t), :])
        for copy in face_copies(p):
            copy.wait_recv()
        faces = orthogonal(fin[p].astype(F32), lambda i: vf[i])
        vf[p] = faces
        faces_b = faces.astype(BF)
        for t in range(tiles):
            tile = al[p, rows(t), :] + dot(ct[rows(t), :], faces_b)
            u[rows(t), :] = tile
            ub[rows(t), :] = tile.astype(BF)
        y_start(p + 1)

    coeffs = least_squares(initial_norm, heights)
    stores = []
    for t in range(tiles):
        tile = coeffs[0] * vs[0, rows(t), :]
        for i in range(1, ITERS):
            tile = tile + coeffs[i] * vs[i, rows(t), :]
        out_v[:, rows(t)] = tile.T
        store = pltpu.make_async_copy(out_v.at[:, rows(t)], out_h.at[:, rows(t)], out_sem.at[t])
        store.start()
        stores.append(store)
    if g > 1:
        ci_wait(0)
    for p in range(ITERS + 1):
        y_wait(p, 0)
        d_wait(p, 0)
        if p < ITERS:
            for copy in face_copies(p):
                copy.wait_send()
    for store in stores:
        store.wait()


def on_device(n, g, rhs, op, od, sv, sd, up, lo, cu, cd, cb, ci):
    nrhs, nloc = rhs.shape
    kc = cb.shape[0]
    face = up.shape[1]
    phases = ITERS + 1
    vmem = pltpu.VMEM
    dma = pltpu.SemaphoreType.DMA
    od, sd = od.reshape(1, nloc), sd.reshape(1, nloc)
    return pl.pallas_call(
        functools.partial(kernel, n, g),
        out_shape=jax.ShapeDtypeStruct(rhs.shape, F32),
        in_specs=[pl.BlockSpec(memory_space=pl.ANY)] * 11,
        out_specs=pl.BlockSpec(memory_space=pl.ANY),
        scratch_shapes=[
            vmem((nrhs, nloc), F32), vmem((nloc, nloc), BF), vmem((1, nloc), F32),
            vmem((nloc, nloc), BF), vmem((1, nloc), F32),
            vmem((1, face), jnp.int32), vmem((1, face), jnp.int32),
            vmem((face, face), BF), vmem((face, face), BF),
            vmem((kc, nloc), BF), vmem((kc, n * kc), BF),
            vmem((nloc, nrhs), F32), vmem((nloc, nrhs), F32),
            vmem((2 * face, nloc), BF), vmem((nloc, 2 * face), BF), vmem((nloc, kc), BF),
            vmem((nloc, nrhs), F32), vmem((nloc, 2 * nrhs), BF),
            vmem((ITERS, nloc, nrhs), F32), vmem((ITERS, nloc, nrhs), F32),
            vmem((nloc, nrhs), F32), vmem((nloc, nrhs), BF), vmem((nloc, nrhs), F32),
            vmem((nrhs, nloc), F32),
            vmem((phases, n * kc, nrhs), BF),
            vmem((ITERS, 2 * face, nrhs), BF), vmem((ITERS, 2 * face, nrhs), BF),
            vmem((ITERS, 2 * face, nrhs), F32), vmem((phases, n * 8, nrhs), F32),
            dma((11,)), dma((nloc // TILE,)), dma((2,)), dma((phases, 2)),
            dma((ITERS, 4)), dma((phases, 2)),
        ],
        compiler_params=pltpu.CompilerParams(
            collective_id=0, has_side_effects=True, vmem_limit_bytes=40 * 1024 * 1024),
    )(rhs, op, od, sv, sd, up, lo, cu, cd, cb, ci)


def solution(mesh):
    return jax.shard_map(
        functools.partial(on_device, mesh.shape["sub"], mesh.shape["grp"]),
        mesh=mesh,
        in_specs=(
            P("grp", "sub"),
            P("sub", None),
            P("sub"),
            P("sub", None),
            P("sub"),
            P("sub", None),
            P("sub", None),
            P("sub", None),
            P("sub", None),
            P(None, "sub"),
            P(("sub", "grp"), None),
        ),
        out_specs=P("grp", "sub"),
        check_vma=False,
    )
```

```python
import functools

import jax
import jax.numpy as jnp
from jax import lax
from jax.experimental import pallas as pl
from jax.experimental.pallas import tpu as pltpu
from jax.sharding import PartitionSpec as P

ITERS = 3
EPS = 1e-06
TILE = 256
MESH = pl.DeviceIdType.MESH
BF = jnp.bfloat16
F32 = jnp.float32


def dot(a, b):
    return jnp.dot(a, b, preferred_element_type=F32)


def least_squares(initial_norm, columns):
    extent = len(columns)
    rotations = []
    target = [initial_norm] + [jnp.zeros_like(initial_norm) for _ in range(extent)]
    triangle = []
    for j in range(extent):
        column = list(columns[j])
        for i in range(j):
            cosine, sine_value = rotations[i]
            leading = cosine * column[i] + sine_value * column[i + 1]
            column[i + 1] = -sine_value * column[i] + cosine * column[i + 1]
            column[i] = leading
        radius = jnp.sqrt(column[j] * column[j] + column[j + 1] * column[j + 1])
        cosine = column[j] / radius
        sine_value = column[j + 1] / radius
        column[j] = radius
        rotations.append((cosine, sine_value))
        target[j + 1] = -sine_value * target[j]
        target[j] = cosine * target[j]
        triangle.append(column[: j + 1])
    coeffs = [None] * extent
    for j in reversed(range(extent)):
        partial_sum = target[j]
        for k in range(j + 1, extent):
            partial_sum = partial_sum - triangle[k][j] * coeffs[k]
        coeffs[j] = partial_sum / triangle[j][j]
    return coeffs


def each_peer(count, body):
    if count <= 8:
        for k in range(1, count):
            body(k)
    else:
        def step(k, carry):
            body(k)
            return carry
        lax.fori_loop(1, count, step, 0)


def kernel(
    n, g, rhs_h, op_h, od_h, sv_h, sd_h, up_h, lo_h, cu_h, cd_h, cb_h, ci_h, out_h,
    rhs_v, op_v, od_v, sv_v, sd_v, up_v, lo_v, cu_v, cd_v, cb_v, ci_v,
    odt, sdt, pg, ct, cbt, w, wb, vs, zs, u, ub, loc, out_v,
    yall, fout, fin, vf, dall, ub2, et, qout, qin, stage, gcol, cout, cin, cs,
    in_sem, out_sem, ci_sem, ysem, fsem, dsem, qsem, gsem, csem,
):
    me = lax.axis_index("sub")
    mg = lax.axis_index("grp")
    nloc = op_v.shape[0]
    kc = cb_v.shape[0]
    face = up_v.shape[1]
    part = ci_h.shape[0]
    tiles = nloc // TILE

    def rows(t):
        return pl.ds(t * TILE, TILE)

    loads = [
        pltpu.make_async_copy(src, dst, in_sem.at[i])
        for i, (src, dst) in enumerate([
            (rhs_h, rhs_v), (cb_h, cb_v), (sv_h, sv_v), (op_h, op_v), (od_h, od_v), (sd_h, sd_v),
            (up_h, up_v), (lo_h, lo_v), (cu_h, cu_v), (cd_h, cd_v),
            (ci_h, ci_v.at[pl.ds(pl.multiple_of(mg * part, part), part)]),
        ])
    ]
    for load in loads:
        load.start()

    barrier = pltpu.get_barrier_semaphore()
    each_peer(n, lambda k: pl.semaphore_signal(
        barrier, inc=1, device_id={"sub": lax.rem(me + k, n)}, device_id_type=MESH))
    each_peer(g, lambda k: pl.semaphore_signal(
        barrier, inc=1, device_id={"grp": lax.rem(mg + k, g)}, device_id_type=MESH))

    loads[0].wait()
    for t in range(tiles):
        tile = rhs_v[:, rows(t)].T
        u[rows(t), :] = tile
        ub[rows(t), :] = tile.astype(BF)
    loads[1].wait()
    loads[10].wait()

    pl.semaphore_wait(barrier, n - 1 + g - 1)

    my_part = pl.ds(pl.multiple_of(mg * part, part), part)

    def send_part(k):
        pltpu.make_async_remote_copy(
            ci_v.at[my_part], ci_v.at[my_part], ci_sem.at[0], ci_sem.at[1],
            device_id={"grp": lax.rem(mg + k, g)}, device_id_type=MESH).start()

    def y_start(p):
        slot = pl.ds(pl.multiple_of(me * kc, kc), kc)
        yall[p, slot, :] = dot(cb_v[...], ub[...]).astype(BF)

        def send(k):
            pltpu.make_async_remote_copy(
                yall.at[p, slot], yall.at[p, slot], ysem.at[p, 0], ysem.at[p, 1],
                device_id={"sub": lax.rem(me + k, n)}, device_id_type=MESH).start()
        each_peer(n, send)

    def y_wait(p, which):
        span = yall.at[p, pl.ds(0, (n - 1) * kc)]
        pltpu.make_async_copy(span, span, ysem.at[p, which]).wait()

    def d_wait(p, which):
        span = dall.at[p, pl.ds(0, (n - 1) * 8)]
        pltpu.make_async_copy(span, span, dsem.at[p, which]).wait()

    def ci_wait(which):
        span = ci_v.at[pl.ds(0, (g - 1) * part)]
        pltpu.make_async_copy(span, span, ci_sem.at[which]).wait()

    def face_copies(p):
        down = {"sub": lax.rem(me + n - 1, n)}
        up = {"sub": lax.rem(me + 1, n)}
        lower = pltpu.make_async_remote_copy(
            fout.at[p, pl.ds(face, face)], fin.at[p, pl.ds(0, face)],
            fsem.at[p, 0], fsem.at[p, 1], device_id=down, device_id_type=MESH)
        upper = pltpu.make_async_remote_copy(
            fout.at[p, pl.ds(0, face)], fin.at[p, pl.ds(face, face)],
            fsem.at[p, 2], fsem.at[p, 3], device_id=up, device_id_type=MESH)
        return lower, upper

    y_start(0)
    each_peer(g, send_part)

    for load in loads[4:10]:
        load.wait()
    for t in range(tiles):
        cols = rows(t)
        cbt[cols, :] = cb_v[:, cols].astype(F32).T.astype(BF)
        position = lax.broadcasted_iota(jnp.int32, (TILE, face), 0) + t * TILE
        for f, (list_v, couple_v) in enumerate(((up_v, cu_v), (lo_v, cd_v))):
            hot = (position == jnp.broadcast_to(list_v[...], (TILE, face))).astype(F32)
            pg[pl.ds(f * face, face), cols] = hot.T.astype(BF)
            ct[cols, pl.ds(f * face, face)] = lax.dot_general(
                hot.astype(BF), couple_v[...], (((1,), (1,)), ((), ())),
                preferred_element_type=F32).astype(BF)
    qboth = dot(cb_v[...], ct[...]).astype(BF)
    qout[pl.ds(0, kc), :] = qboth[:, face:]
    qout[pl.ds(kc, kc), :] = qboth[:, :face]
    q_copies = (
        pltpu.make_async_remote_copy(
            qout.at[pl.ds(0, kc)], qin.at[pl.ds(0, kc)], qsem.at[0], qsem.at[1],
            device_id={"sub": lax.rem(me + n - 1, n)}, device_id_type=MESH),
        pltpu.make_async_remote_copy(
            qout.at[pl.ds(kc, kc)], qin.at[pl.ds(kc, kc)], qsem.at[2], qsem.at[3],
            device_id={"sub": lax.rem(me + 1, n)}, device_id_type=MESH),
    )
    for copy in q_copies:
        copy.start()
    for t in range(tiles):
        cols = rows(t)
        sdt[cols, :] = jnp.broadcast_to(sd_v[:, cols], (128, TILE)).T
    loads[2].wait()
    for t in range(tiles):
        loc[rows(t), :] = sdt[rows(t), :] * u[rows(t), :] + dot(sv_v[rows(t), :], ub[...])

    if g > 1:
        ci_wait(1)
    my_rows = pl.ds(pl.multiple_of(me * kc, kc), kc)
    for s in range(n):
        for i in range(3):
            block = (s + i - 1 + n) % n
            stage[s, :, pl.ds(i * kc, kc)] = ci_v[:, pl.ds(block * kc, kc)]
        stage[s, :, pl.ds(3 * kc, kc)] = jnp.zeros((kc, kc), BF)

    def send_columns(k):
        to = lax.rem(me + k, n)
        pltpu.make_async_remote_copy(
            stage.at[to], gcol.at[my_rows], gsem.at[0], gsem.at[1],
            device_id={"sub": to}, device_id_type=MESH).start()
    each_peer(n, send_columns)
    gcol[my_rows, :] = stage[me]

    def g_wait(which):
        span = gcol.at[pl.ds(0, (n - 1) * kc)]
        pltpu.make_async_copy(span, span, gsem.at[which]).wait()

    def c_wait(p, which):
        span = cin.at[p, pl.ds(0, (n - 1) * kc)]
        pltpu.make_async_copy(span, span, csem.at[p, which]).wait()

    for t in range(tiles):
        cols = rows(t)
        odt[cols, :] = jnp.broadcast_to(od_v[:, cols], (128, TILE)).T
        diag = sdt[cols, :]
        diag = jnp.concatenate([diag] * (2 * face // 128), axis=1)
        et[cols, :] = (diag * ct[cols, :].astype(F32) + dot(sv_v[cols, :], ct[...])).astype(BF)

    y_wait(0, 1)
    c = dot(ci_v[...], yall[0]).astype(BF)
    for t in range(tiles):
        w[rows(t), :] = loc[rows(t), :] + dot(cbt[rows(t), :], c)

    heights = []
    gram = {}
    initial_norm = None
    for j in range(-1, ITERS):
        p = j + 1
        last = j == ITERS - 1
        sums = [None] * (2 * p + 1)
        for t in range(tiles):
            tile = w[rows(t), :]
            if not last:
                high = tile.astype(BF)
                wb[rows(t), 0:128] = high
                wb[rows(t), 128:256] = (tile - high.astype(F32)).astype(BF)
            pairs = [(tile, tile)]
            basis = [vs[i, rows(t), :] for i in range(p)]
            pairs += [(tile, b) for b in basis]
            pairs += [(basis[p - 1], b) for b in basis]
            for i, (a, b) in enumerate(pairs):
                one = jnp.sum((a * b).reshape(TILE // 8, 8, 128), axis=0)
                sums[i] = one if sums[i] is None else sums[i] + one
        packed = [jnp.sum(s, axis=0, keepdims=True) for s in sums]
        packed += [jnp.zeros((8 - len(packed), 128), F32)]
        slot = pl.ds(pl.multiple_of(me * 8, 8), 8)
        dall[p, slot, :] = jnp.concatenate(packed, axis=0)

        def send_dots(k):
            pltpu.make_async_remote_copy(
                dall.at[p, slot], dall.at[p, slot], dsem.at[p, 0], dsem.at[p, 1],
                device_id={"sub": lax.rem(me + k, n)}, device_id_type=MESH).start()
        each_peer(n, send_dots)

        if not last:
            fout[p] = dot(pg[...], wb[:, 0:128]).astype(BF)
            for copy in face_copies(p):
                copy.start()
            if p == 0:
                loads[3].wait()
            for t in range(tiles):
                both = dot(op_v[rows(t), :], wb[...])
                tile = odt[rows(t), :] * w[rows(t), :] + (both[:, :128] + both[:, 128:])
                u[rows(t), :] = tile
                high = tile.astype(BF)
                ub2[rows(t), 0:128] = high
                ub2[rows(t), 128:256] = (tile - high.astype(F32)).astype(BF)
            if p == 0:
                for copy in q_copies:
                    copy.wait_recv()
                g_wait(1)
            shares = jnp.concatenate([
                dot(qin[pl.ds(kc, kc), :], fout[p, pl.ds(face, face), :]),
                dot(cb_v[...], ub2[:, 0:128]),
                dot(qin[pl.ds(0, kc), :], fout[p, pl.ds(0, face), :]),
                jnp.zeros((kc, 128), F32)], axis=0).astype(BF)
            cout[p] = dot(gcol[...], shares).astype(BF)

            def send_share(k):
                to = lax.rem(me + k, n)
                theirs = pl.ds(pl.multiple_of(to * kc, kc), kc)
                pltpu.make_async_remote_copy(
                    cout.at[p, theirs], cin.at[p, my_rows], csem.at[p, 0], csem.at[p, 1],
                    device_id={"sub": to}, device_id_type=MESH).start()
            each_peer(n, send_share)
            cin[p, my_rows, :] = cout[p, my_rows, :]
            for t in range(tiles):
                both = dot(sv_v[rows(t), :], ub2[...])
                zs[p, rows(t), :] = sdt[rows(t), :] * u[rows(t), :] + (both[:, :128] + both[:, 128:])

        d_wait(p, 1)
        total = jnp.sum(dall[p].reshape(n, 8, 128), axis=0)
        square = total[0:1, :]
        h = [total[1 + i:2 + i, :] for i in range(p)]
        for i in range(p):
            gram[i, p - 1] = gram[p - 1, i] = total[1 + p + i:2 + p + i, :]
        for i in range(p):
            square = square - 2.0 * h[i] * h[i]
            for k in range(p):
                square = square + h[i] * h[k] * gram[i, k]
        norm = jnp.sqrt(jnp.maximum(square, 0.0) + EPS)
        if p == 0:
            initial_norm = norm
        else:
            heights.append(h + [norm])
        if last:
            break
        scale = 1.0 / norm

        def orthogonal(value, earlier):
            for i in range(p):
                value = value - h[i] * earlier(i)
            return value * scale

        for t in range(tiles):
            vs[p, rows(t), :] = orthogonal(w[rows(t), :], lambda i: vs[i, rows(t), :])
            zs[p, rows(t), :] = orthogonal(zs[p, rows(t), :], lambda i: zs[i, rows(t), :])
        for copy in face_copies(p):
            copy.wait_recv()
        faces = orthogonal(fin[p].astype(F32), lambda i: vf[i])
        vf[p] = faces
        faces_b = faces.astype(BF)
        c_wait(p, 1)
        coarse = jnp.sum(cin[p].astype(F32).reshape(n, kc, 128), axis=0)
        coarse = orthogonal(coarse, lambda i: cs[i])
        cs[p] = coarse
        coarse_b = coarse.astype(BF)
        for t in range(tiles):
            w[rows(t), :] = zs[p, rows(t), :] + (
                dot(et[rows(t), :], faces_b) + dot(cbt[rows(t), :], coarse_b))

    coeffs = least_squares(initial_norm, heights)
    stores = []
    for t in range(tiles):
        tile = coeffs[0] * vs[0, rows(t), :]
        for i in range(1, ITERS):
            tile = tile + coeffs[i] * vs[i, rows(t), :]
        out_v[:, rows(t)] = tile.T
        store = pltpu.make_async_copy(out_v.at[:, rows(t)], out_h.at[:, rows(t)], out_sem.at[t])
        store.start()
        stores.append(store)
    if g > 1:
        ci_wait(0)
    y_wait(0, 0)
    g_wait(0)
    for copy in q_copies:
        copy.wait_send()
    for p in range(ITERS + 1):
        d_wait(p, 0)
        if p < ITERS:
            c_wait(p, 0)
            for copy in face_copies(p):
                copy.wait_send()
    for store in stores:
        store.wait()


def on_device(n, g, rhs, op, od, sv, sd, up, lo, cu, cd, cb, ci):
    nrhs, nloc = rhs.shape
    kc = cb.shape[0]
    face = up.shape[1]
    phases = ITERS + 1
    vmem = pltpu.VMEM
    dma = pltpu.SemaphoreType.DMA
    od, sd = od.reshape(1, nloc), sd.reshape(1, nloc)
    return pl.pallas_call(
        functools.partial(kernel, n, g),
        out_shape=jax.ShapeDtypeStruct(rhs.shape, F32),
        in_specs=[pl.BlockSpec(memory_space=pltpu.HBM)] * 11,
        out_specs=pl.BlockSpec(memory_space=pltpu.HBM),
        scratch_shapes=[
            vmem((nrhs, nloc), F32), vmem((nloc, nloc), BF), vmem((1, nloc), F32),
            vmem((nloc, nloc), BF), vmem((1, nloc), F32),
            vmem((1, face), jnp.int32), vmem((1, face), jnp.int32),
            vmem((face, face), BF), vmem((face, face), BF),
            vmem((kc, nloc), BF), vmem((kc, n * kc), BF),
            vmem((nloc, nrhs), F32), vmem((nloc, nrhs), F32),
            vmem((2 * face, nloc), BF), vmem((nloc, 2 * face), BF), vmem((nloc, kc), BF),
            vmem((nloc, nrhs), F32), vmem((nloc, 2 * nrhs), BF),
            vmem((ITERS, nloc, nrhs), F32), vmem((ITERS, nloc, nrhs), F32),
            vmem((nloc, nrhs), F32), vmem((nloc, nrhs), BF), vmem((nloc, nrhs), F32),
            vmem((nrhs, nloc), F32),
            vmem((1, n * kc, nrhs), BF),
            vmem((ITERS, 2 * face, nrhs), BF), vmem((ITERS, 2 * face, nrhs), BF),
            vmem((ITERS, 2 * face, nrhs), F32), vmem((phases, n * 8, nrhs), F32),
            vmem((nloc, 2 * nrhs), BF), vmem((nloc, 2 * face), BF),
            vmem((2 * kc, face), BF), vmem((2 * kc, face), BF),
            vmem((n, kc, 4 * kc), BF), vmem((n * kc, 4 * kc), BF),
            vmem((ITERS, n * kc, nrhs), BF), vmem((ITERS, n * kc, nrhs), BF),
            vmem((ITERS, kc, nrhs), F32),
            dma((11,)), dma((nloc // TILE,)), dma((2,)), dma((1, 2)),
            dma((ITERS, 4)), dma((phases, 2)), dma((4,)), dma((2,)), dma((ITERS, 2)),
        ],
        compiler_params=pltpu.CompilerParams(
            collective_id=0, has_side_effects=True, vmem_limit_bytes=64 * 1024 * 1024 - 65536),
    )(rhs, op, od, sv, sd, up, lo, cu, cd, cb, ci)


def solution(mesh):
    return jax.shard_map(
        functools.partial(on_device, mesh.shape["sub"], mesh.shape["grp"]),
        mesh=mesh,
        in_specs=(
            P("grp", "sub"),
            P("sub", None),
            P("sub"),
            P("sub", None),
            P("sub"),
            P("sub", None),
            P("sub", None),
            P("sub", None),
            P("sub", None),
            P(None, "sub"),
            P(("sub", "grp"), None),
        ),
        out_specs=P("grp", "sub"),
        check_vma=False,
    )
```
